32 devices in a mesh: groups: 2 (over x), wide: 16 (over z, y, core).
Axes of the slice: x: 2, y: 2, z: 4, core: 2. Of those that a mesh axis runs over, the one named last changes fastest.
Arguments:
- doc_len: int32 [256], P('groups'), parts along dimension 0, may hold values from 1 to 505, as said below
- doc_owner: int32 [256], P('groups'), parts along dimension 0, may hold values from 0 to 127, each once
- query_act: bfloat16 [256, 4096], P('groups'), parts along dimension 0, may hold values from -0.09375 to 0.09375
- query_grad: bfloat16 [256, 7168], P('groups'), parts along dimension 0, may hold values from -0.0625 to 0.0625
- basis_act: bfloat16 [8192, 4096], P('groups', 'wide'), parts along dimension 0, may hold values from -0.09375 to 0.09375
- basis_grad: bfloat16 [14336, 7168], P('groups', 'wide'), parts along dimension 0, may hold values from -0.0625 to 0.0625
- eig_act: float32 [8192], P(('groups', 'wide')), parts along dimension 0, may hold values from 0.02 to 5
- eig_grad: float32 [14336], P(('groups', 'wide')), parts along dimension 0, may hold values from 0.02 to 5
- token_act: bfloat16 [16384, 4096], P(('groups', 'wide')), parts along dimension 0, may hold values from -6 to 6
- token_grad: bfloat16 [16384, 7168], P(('groups', 'wide')), parts along dimension 0, may hold values from -6 to 6
Outputs:
- scores: float32 [256, 64], P(('groups', 'wide')), parts along dimension 0
The draws below stay inside these ranges and needn't reach their ends.
There are 2 independent parts, one for each index of `groups`. The reference program is written for one: setup_inputs(seed, part) draws one part's arguments, and reference() takes and returns one part's arrays. A program takes and returns all parts, laid end to end along the dimension named above; each array names one. Nothing has to cross between parts.
Inputs may be any that keep to these rules, and one draw needn't show every extreme that they name: `doc_len`: each device's 8 lengths are at least 1 and sum to 16 times a whole number from 1 to 32; the devices' sums add up to 4224, and on some device the sum is 512, with one document of 505 rows.
All inputs are finite; a program needn't handle non-finite values.
Results may differ from the reference program's by a relative error of at most 0.0003.
Values may be sent and summed in bfloat16 or wider, within the bound.
A program may use at most 128 MiB of HBM per device.

```python
import math
import jax
import jax.numpy as jnp
from jax import lax

D = 4096
FW = 7168
NQ = 64
RANK = 2
TOK_DEV = 512
DOC_DEV = 8
QROWS = 128
TOKENS = 8192
DOCS_ALL = 128
N_WIDE = 16


def draw_doc_len(key, part):
    key = jax.random.fold_in(key, 11)
    key_low, key_order, key_cuts = jax.random.split(key, 3)
    most = TOK_DEV // N_WIDE
    half = N_WIDE // 2
    lower = jax.random.randint(key_low, (half,), 1, most + 1)
    lower = lower.at[0].set(most)
    paired = jnp.concatenate([lower, most + 1 - lower])
    order = jax.random.permutation(key_order, N_WIDE)
    blocks = paired[order]
    live = blocks * N_WIDE
    position = jnp.arange(1, TOK_DEV)
    noise = jax.random.randint(key_cuts, (N_WIDE, TOK_DEV - 1), 0, TOK_DEV)
    ranked = jnp.where(position[None, :] < live[:, None], noise * TOK_DEV + position[None, :], -position[None, :])
    forced = (order == 0)[:, None]
    ranked = jnp.where(forced, TOK_DEV * TOK_DEV - position[None, :], ranked)
    chosen = lax.top_k(ranked, DOC_DEV - 1)[0]
    cuts = jnp.sort(chosen % TOK_DEV, axis=1)
    edges = jnp.concatenate([jnp.zeros((N_WIDE, 1), jnp.int32), cuts.astype(jnp.int32), live[:, None].astype(jnp.int32)], axis=1)
    return (edges[:, 1:] - edges[:, :-1]).reshape(-1).astype(jnp.int32)


def levels(key, extent, pieces, low, largest):
    factor_of, own = 1.0, jax.random.fold_in(key, 6)
    for axis_at, shards_of in pieces:
        heights = jnp.exp(jax.random.uniform(jax.random.fold_in(own, axis_at), (shards_of,), jnp.float32, low / len(pieces), largest / len(pieces)))
        factor_of = factor_of * jnp.repeat(heights, extent[axis_at] // shards_of).reshape([-1 if axis == axis_at else 1 for axis in range(len(extent))])
    return factor_of


def normal_values(own_key, dims, spread, limit, shards=(), held_as=jnp.bfloat16):
    gain = levels(own_key, dims, shards, -0.22, 0.18) if shards else 1.0
    result = jax.random.normal(own_key, dims, jnp.float32) * spread * gain
    return jnp.minimum(jnp.maximum(result, -limit), limit).astype(held_as)


def setup_inputs(seed: int = 0, part: int = 0) -> dict:
    splits = jax.random.split(jax.random.key(seed), 11)
    part_keys = jax.random.split(jax.random.fold_in(splits[10], part), 11)
    return {
        "doc_len": draw_doc_len(jax.random.fold_in(jax.random.fold_in(splits[10], part), 71), part),
        "doc_owner": jax.random.permutation(part_keys[1], DOCS_ALL).astype(jnp.int32),
        "query_act": normal_values(part_keys[2], (QROWS, D), D ** -0.5, 0.09375),
        "query_grad": normal_values(part_keys[3], (QROWS, FW), FW ** -0.5, 0.0625),
        "basis_act": normal_values(part_keys[4], (D, D), D ** -0.5, 0.09375, ((1, 16),)),
        "basis_grad": normal_values(part_keys[5], (FW, FW), FW ** -0.5, 0.0625, ((1, 16),)),
        "eig_act": jnp.clip(jnp.exp(math.log(5.0) - 5.521461 * jax.random.uniform(part_keys[6], (D,), jnp.float32) ** levels(part_keys[6], (D,), ((0, 16),), -0.2, 0.2)), 0.02, 5.0),
        "eig_grad": jnp.clip(jnp.exp(math.log(5.0) - 5.521461 * jax.random.uniform(part_keys[7], (FW,), jnp.float32) ** levels(part_keys[7], (FW,), ((0, 16),), -0.2, 0.2)), 0.02, 5.0),
        "token_act": normal_values(part_keys[8], (TOKENS, D), 1.0, 6.0, ((0, 16),)),
        "token_grad": normal_values(part_keys[9], (TOKENS, FW), 1.0, 6.0, ((0, 16),)),
    }


DAMP = 0.1


def damped(query, basis, eigen):
    coords = jnp.dot(query, basis, preferred_element_type=jnp.float32) * (1.0 / (eigen + DAMP))
    return jnp.dot(coords, basis.astype(jnp.float32).T, precision=lax.Precision.HIGHEST, preferred_element_type=jnp.float32)


def reference(doc_len, doc_owner, query_act, query_grad, basis_act, basis_grad, eig_act, eig_grad, token_act, token_grad):
    hat_act = damped(query_act, basis_act, eig_act)
    hat_grad = damped(query_grad, basis_grad, eig_grad)
    prod_act = jnp.dot(hat_act, token_act.astype(jnp.float32).T, precision=lax.Precision.HIGHEST, preferred_element_type=jnp.float32)
    prod_grad = jnp.dot(hat_grad, token_grad.astype(jnp.float32).T, precision=lax.Precision.HIGHEST, preferred_element_type=jnp.float32)
    token_score = (prod_act * prod_grad).reshape(NQ, RANK, TOKENS).sum(axis=1)
    table = doc_len.reshape(N_WIDE, DOC_DEV)
    ends = jnp.cumsum(table, axis=1)
    place = jnp.arange(TOK_DEV).astype(jnp.int32)
    within = jnp.sum((place[None, :, None] >= ends[:, None, :]).astype(jnp.int32), axis=2)
    within = jnp.minimum(within, DOC_DEV - 1)
    live = place[None, :] < ends[:, DOC_DEV - 1:]
    global_doc = (jnp.arange(N_WIDE).astype(jnp.int32)[:, None] * DOC_DEV + within).reshape(-1)
    length = doc_len[global_doc].astype(jnp.float32)
    owner = doc_owner[global_doc]
    weight = jnp.where(live.reshape(-1), 1.0 / length, jnp.float32(0.0))
    weighted = (token_score * weight[None, :]).T
    return jax.ops.segment_sum(weighted, owner, num_segments=DOCS_ALL)
```

```python
import functools

import jax
import jax.numpy as jnp
from jax import lax
from jax.experimental import pallas as pl
from jax.experimental.pallas import tpu as pltpu
from jax.sharding import PartitionSpec as P

RANK = 2
DAMP = 0.1
LANES = 128
LEVELS = 32767.0
LEAST = 1e-34
MESH = pl.DeviceIdType.MESH


def remote(src, dst, send, recv, there):
    return pltpu.make_async_remote_copy(
        src_ref=src, dst_ref=dst, send_sem=send, recv_sem=recv, device_id=there, device_id_type=MESH
    )


def quantize(x):
    most = jnp.max(jnp.abs(x), axis=0, keepdims=True)
    up = jnp.where(most > LEAST, LEVELS / jnp.maximum(most, LEAST), 0.0)
    return jnp.round(x * up).astype(jnp.int32).astype(jnp.int16), most * (1.0 / LEVELS)


def dequantize(q, scale):
    return q.astype(jnp.int32).astype(jnp.float32) * scale


def reduce_kernel(
    shape,
    part_ref,
    out_ref,
    core_in,
    y_out,
    y_out_s,
    y_in,
    y_in_s,
    z_out,
    z_out_s,
    z_in,
    z_in_s,
    hat,
    hat_s,
    core_sem,
    y_sem,
    z_sem,
    az_sem,
    ay_sem,
    ac_sem,
):
    A, B, K, R, W = shape
    g = lax.axis_index("groups")
    me = lax.axis_index("wide")
    core = lax.rem(me, 2)
    b = lax.rem(me // 2, B)
    a = me // (2 * B)
    other = 1 - core
    strips = W // LANES

    def device(a_, b_, core_):
        return (g, (a_ * B + b_) * 2 + core_)

    peer = device(a, b, other)
    ys = [device(a, lax.rem(b + i, B), core) for i in range(B)]
    zs = [device(lax.rem(a + j, A), b, core) for j in range(A)]

    barrier = pltpu.get_barrier_semaphore()
    for there in [peer] + ys[1:] + zs[1:]:
        pl.semaphore_signal(barrier, inc=1, device_id=there, device_id_type=MESH)
    pl.semaphore_wait(barrier, 1 + (B - 1) + (A - 1))

    def column(core_, b_, k):
        return pl.multiple_of(((core_ * B + b_) * K + k) * W, LANES)

    def lanes(at, t):
        return pl.ds(pl.multiple_of(at + t * LANES, LANES), LANES)

    def strip_loop(body):
        def run(t, carry):
            body(t)
            return carry

        lax.fori_loop(0, strips, run, 0)

    started = []

    def go(copy):
        copy.start()
        started.append(copy)
        return copy

    def go_pair(q_src, q_dst, s_src, s_dst, sems, at, there):
        q = go(remote(q_src, q_dst, sems.at[(0, 0) + at], sems.at[(1, 0) + at], there))
        s = go(remote(s_src, s_dst, sems.at[(0, 1) + at], sems.at[(1, 1) + at], there))
        return q, s

    order = [i for i in range(1, B)] + [0]
    core_copies = {}
    for k in range(K):
        for i in order:
            bb = lax.rem(b + i, B)
            core_copies[k, i] = go(
                remote(
                    part_ref.at[:, pl.ds(column(other, bb, k), W)],
                    core_in.at[i, k],
                    core_sem.at[0, i, k],
                    core_sem.at[1, i, k],
                    peer,
                )
            )

    y_copies = {}
    for k in range(K):
        for i in range(1, B):
            at = column(core, lax.rem(b + i, B), k)
            core_copies[k, i].wait_recv()

            def send_y(t, at=at, i=i, k=k):
                q, s = quantize(part_ref[:, lanes(at, t)] + core_in[i, k, :, lanes(0, t)])
                y_out[i - 1, k, :, lanes(0, t)] = q
                y_out_s[i - 1, k, :, lanes(0, t)] = s

            strip_loop(send_y)
            y_copies[k, i] = go_pair(
                y_out.at[i - 1, k],
                y_in.at[i - 1, k],
                y_out_s.at[i - 1, k],
                y_in_s.at[i - 1, k],
                y_sem,
                (i - 1, k),
                ys[i],
            )

    z_copies = {}
    for k in range(K):
        core_copies[k, 0].wait_recv()
        for i in range(1, B):
            for c in y_copies[k, i]:
                c.wait_recv()
        at = column(core, b, k)

        def add_y(t, at=at, k=k):
            total = part_ref[:, lanes(at, t)] + core_in[0, k, :, lanes(0, t)]
            for i in range(1, B):
                total = total + dequantize(y_in[i - 1, k, :, lanes(0, t)], y_in_s[i - 1, k, :, lanes(0, t)])
            core_in[0, k, :, lanes(0, t)] = total
            for v in range(A):
                q, s = quantize(total[v * R : (v + 1) * R])
                z_out[k, v, :, lanes(0, t)] = q
                z_out_s[k, v, :, lanes(0, t)] = s

        strip_loop(add_y)
        for j in range(1, A):
            aa = lax.rem(a + j, A)
            z_copies[k, j] = go_pair(
                z_out.at[k, aa],
                z_in.at[k, j - 1],
                z_out_s.at[k, aa],
                z_in_s.at[k, j - 1],
                z_sem,
                (k, j - 1),
                zs[j],
            )

    az, ay, ac = {}, {}, {}

    def push(sems, at, there, where):
        return go_pair(hat.at[where], hat.at[where], hat_s.at[where], hat_s.at[where], sems, at, there)

    for k in range(K):
        for j in range(1, A):
            for c in z_copies[k, j]:
                c.wait_recv()
        rows = pl.ds(pl.multiple_of(a * R, R), R)

        def add_z(t, k=k, rows=rows):
            total = core_in[0, k, rows, lanes(0, t)]
            for j in range(1, A):
                total = total + dequantize(z_in[k, j - 1, :, lanes(0, t)], z_in_s[k, j - 1, :, lanes(0, t)])
            q, s = quantize(total)
            hat[core, b, k, a, :, lanes(0, t)] = q
            hat_s[core, b, k, a, :, lanes(0, t)] = s

        strip_loop(add_z)
        where = (core, b, k, a)
        for j in range(1, A):
            az[k, j] = push(az_sem, (k, j - 1), zs[j], where)
        for i in range(1, B):
            ay[k, i, 0] = push(ay_sem, (k, i - 1, 0), ys[i], where)
        ac[k, 0, 0] = push(ac_sem, (k, 0, 0), peer, where)

    for k in range(K):
        for j in range(1, A):
            for c in az[k, j]:
                c.wait_recv()
            where = (core, b, k, lax.rem(a - j + A, A))
            for i in range(1, B):
                ay[k, i, j] = push(ay_sem, (k, i - 1, j), ys[i], where)
            ac[k, 0, j] = push(ac_sem, (k, 0, j), peer, where)
        for i in range(1, B):
            for j in range(A):
                for c in ay[k, i, j]:
                    c.wait_recv()
                where = (core, lax.rem(b - i + B, B), k, lax.rem(a - j + A, A))
                ac[k, i, j] = push(ac_sem, (k, i, j), peer, where)

    for pair in ac.values():
        for c in pair:
            c.wait_recv()

    half = out_ref.shape[0] // 2
    for h in range(2):
        for bb in range(B):
            for k in range(K):

                def unpack(t, h=h, bb=bb, k=k):
                    at = lanes(((h * B + bb) * K + k) * W, t)
                    for v in range(A):
                        value = dequantize(hat[h, bb, k, v, :, lanes(0, t)], hat_s[h, bb, k, v, :, lanes(0, t)])
                        high = value.astype(jnp.bfloat16)
                        out_ref[v * R : (v + 1) * R, at] = high
                        out_ref[half + v * R : half + (v + 1) * R, at] = (
                            value - high.astype(jnp.float32)
                        ).astype(jnp.bfloat16)

                strip_loop(unpack)

    for c in started:
        c.wait_send()


def sum_everywhere(part, n):
    rows, columns = part.shape
    B = 2 if n <= 16 else 4
    A = n // (2 * B)
    R = rows // A
    tiles = columns // (2 * B * LANES)
    K = 2 if tiles % 2 == 0 else 1
    W = columns // (2 * B * K)
    f32, i16 = jnp.float32, jnp.int16
    dma = pltpu.SemaphoreType.DMA
    return pl.pallas_call(
        functools.partial(reduce_kernel, (A, B, K, R, W)),
        out_shape=jax.ShapeDtypeStruct((2 * rows, columns), jnp.bfloat16),
        in_specs=[pl.BlockSpec(memory_space=pltpu.VMEM)],
        out_specs=pl.BlockSpec(memory_space=pltpu.VMEM),
        scratch_shapes=[
            pltpu.VMEM((B, K, rows, W), f32),
            pltpu.VMEM((B - 1, K, rows, W), i16),
            pltpu.VMEM((B - 1, K, 1, W), f32),
            pltpu.VMEM((B - 1, K, rows, W), i16),
            pltpu.VMEM((B - 1, K, 1, W), f32),
            pltpu.VMEM((K, A, R, W), i16),
            pltpu.VMEM((K, A, 1, W), f32),
            pltpu.VMEM((K, A - 1, R, W), i16),
            pltpu.VMEM((K, A - 1, 1, W), f32),
            pltpu.VMEM((2, B, K, A, R, W), i16),
            pltpu.VMEM((2, B, K, A, 1, W), f32),
            dma((2, B, K)),
            dma((2, 2, B - 1, K)),
            dma((2, 2, K, A - 1)),
            dma((2, 2, K, A - 1)),
            dma((2, 2, K, B - 1, A)),
            dma((2, 2, K, B, A)),
        ],
        compiler_params=pltpu.CompilerParams(
            collective_id=0, has_side_effects=True, vmem_limit_bytes=48 * 1024 * 1024
        ),
    )(part)


def share_kernel(n, mine_ref, owner_ref, out_ref, every, send_sem, recv_sem):
    g = lax.axis_index("groups")
    me = lax.axis_index("wide")
    docs = mine_ref.shape[0]
    barrier = pltpu.get_barrier_semaphore()

    def greet(j, carry):
        pl.semaphore_signal(barrier, inc=1, device_id=(g, lax.rem(me + j, n)), device_id_type=MESH)
        return carry

    lax.fori_loop(1, n, greet, 0)
    pl.semaphore_wait(barrier, n - 1)
    every[me] = mine_ref[...]

    def copy(j):
        return remote(
            mine_ref, every.at[me], send_sem.at[j - 1], recv_sem.at[j - 1], (g, lax.rem(me + j, n))
        )

    def start(j, carry):
        copy(j).start()
        return carry

    def finish(j, carry):
        copy(j).wait()
        return carry

    lax.fori_loop(1, n, start, 0)
    lax.fori_loop(1, n, finish, 0)
    table = every[...].reshape(n * docs, mine_ref.shape[1])
    row = lax.broadcasted_iota(jnp.int32, (docs, n * docs), 0) + me * docs
    pick = (row == owner_ref[...]).astype(jnp.float32)
    out_ref[...] = jnp.dot(
        pick, table, precision=lax.Precision.HIGHEST, preferred_element_type=jnp.float32
    )


def share(mine, owners, n):
    docs, queries = mine.shape
    return pl.pallas_call(
        functools.partial(share_kernel, n),
        out_shape=jax.ShapeDtypeStruct((docs, queries), jnp.float32),
        in_specs=[pl.BlockSpec(memory_space=pltpu.VMEM)] * 2,
        out_specs=pl.BlockSpec(memory_space=pltpu.VMEM),
        scratch_shapes=[
            pltpu.VMEM((n, docs, queries), jnp.float32),
            pltpu.SemaphoreType.DMA((n - 1,)),
            pltpu.SemaphoreType.DMA((n - 1,)),
        ],
        compiler_params=pltpu.CompilerParams(collective_id=1, has_side_effects=True),
    )(mine, owners)


def split(x):
    high = lax.reduce_precision(x, 8, 7)
    return jnp.concatenate([high, x - high], axis=0).astype(jnp.bfloat16)


def joined(stacked):
    half = stacked.shape[0] // 2
    return stacked[:half] + stacked[half:]


def partial_hat(query, basis, eig, size):
    coords = jnp.dot(query, basis, preferred_element_type=jnp.float32) * (1.0 / (eig + DAMP)) * (1.0 / size)
    back = (((1,), (1,)), ((), ()))
    return joined(lax.dot_general(split(coords), basis, back, preferred_element_type=jnp.float32))


def row_size(query):
    most = jnp.max(jnp.abs(query), axis=1, keepdims=True).astype(jnp.float32)
    return jnp.where(most > 0, most, 1.0)


def shards(
    doc_len,
    doc_owner,
    query_act,
    query_grad,
    basis_act,
    basis_grad,
    eig_act,
    eig_grad,
    token_act,
    token_grad,
):
    n = lax.axis_size("wide")
    me = lax.axis_index("wide")
    width_act = query_act.shape[1]
    size_act, size_grad = row_size(query_act), row_size(query_grad)
    part = jnp.concatenate(
        [
            partial_hat(query_act, basis_act, eig_act, size_act),
            partial_hat(query_grad, basis_grad, eig_grad, size_grad),
        ],
        axis=1,
    )
    hat = sum_everywhere(part, n)

    docs = doc_len.shape[0] // n
    lengths = lax.dynamic_slice(doc_len, (me * docs,), (docs,))
    ends = jnp.sum(jnp.where(jnp.arange(docs)[:, None] >= jnp.arange(docs)[None, :], lengths[None, :], 0), axis=1)
    place = jnp.arange(token_act.shape[0])
    inside = (place[None, :] < ends[:, None]) & (place[None, :] >= (ends - lengths)[:, None])
    member = jnp.where(inside, (1.0 / lengths.astype(jnp.float32))[:, None], 0.0)

    inner = (((1,), (1,)), ((), ()))
    prod_act = joined(
        lax.dot_general(hat[:, :width_act], token_act, inner, preferred_element_type=jnp.float32)
    )
    prod_grad = joined(
        lax.dot_general(hat[:, width_act:], token_grad, inner, preferred_element_type=jnp.float32)
    )
    products = (prod_act * size_act) * (prod_grad * size_grad)
    scores = products.reshape(-1, RANK, products.shape[1]).sum(axis=1)
    mine = lax.dot_general(
        member, scores, inner, precision=lax.Precision.HIGHEST, preferred_element_type=jnp.float32
    )
    return share(mine, doc_owner[None, :], n)


def solution(mesh):
    placed = (
        P("groups"),
        P("groups"),
        P("groups", None),
        P("groups", None),
        P("groups", "wide"),
        P("groups", "wide"),
        P(("groups", "wide")),
        P(("groups", "wide")),
        P(("groups", "wide"), None),
        P(("groups", "wide"), None),
    )
    return jax.shard_map(
        shards, mesh=mesh, in_specs=placed, out_specs=P(("groups", "wide"), None), check_vma=False
    )
```

```python
import functools

import jax
import jax.numpy as jnp
from jax import lax
from jax.experimental import pallas as pl
from jax.experimental.pallas import tpu as pltpu
from jax.sharding import PartitionSpec as P

RANK = 2
DAMP = 0.1
LANES = 128
LEVELS = 32767.0
LEAST = 1e-34
PIECE = 1024
MOST_TILES = 4
MESH = pl.DeviceIdType.MESH


def remote(src, dst, send, recv, there):
    return pltpu.make_async_remote_copy(
        src_ref=src, dst_ref=dst, send_sem=send, recv_sem=recv, device_id=there, device_id_type=MESH
    )


def quantize(x):
    most = jnp.max(jnp.abs(x), axis=0, keepdims=True)
    up = jnp.where(most > LEAST, LEVELS / jnp.maximum(most, LEAST), 0.0)
    return jnp.round(x * up).astype(jnp.int32).astype(jnp.int16), most * (1.0 / LEVELS)


def dequantize(q, scale):
    return q.astype(jnp.int32).astype(jnp.float32) * scale


def chunks_of(tiles_act, tiles_grad, most):
    chunks, lane = [], 0
    for kind, tiles in ((0, tiles_act), (1, tiles_grad)):
        pieces = -(-tiles // most)
        sizes = [tiles // pieces + (1 if p < tiles % pieces else 0) for p in range(pieces)]
        offset = 0
        for size in sizes:
            chunks.append((kind, offset * LANES, lane * LANES, size * LANES))
            offset += size
            lane += size
    return chunks


def kernel(
    shape,
    chunks,
    len_ref,
    owner_ref,
    eig_act_ref,
    eig_grad_ref,
    query_act_hbm,
    query_grad_hbm,
    basis_act_hbm,
    basis_grad_hbm,
    token_act_hbm,
    token_grad_hbm,
    out_ref,
    query_act,
    query_grad,
    basis_act,
    basis_grad,
    token_act,
    token_grad,
    coords_act,
    coords_grad,
    part,
    core_in,
    y_out,
    y_out_s,
    y_in,
    y_in_s,
    z_out,
    z_out_s,
    z_in,
    z_in_s,
    hat,
    hat_s,
    prods,
    mine,
    every,
    load_sem,
    basis_sem,
    core_sem,
    y_sem,
    z_sem,
    az_sem,
    ay_sem,
    ac_sem,
    share_sem,
):
    n, A, B, R = shape
    K = len(chunks)
    rows = A * R
    f32, bf16 = jnp.float32, jnp.bfloat16
    g = lax.axis_index("groups")
    me = lax.axis_index("wide")
    core = lax.rem(me, 2)
    b = lax.rem(me // 2, B)
    a = me // (2 * B)
    other = 1 - core
    queries = (query_act, query_grad)
    bases = (basis_act, basis_grad)
    tokens = (token_act, token_grad)
    coords = (coords_act, coords_grad)
    eigs = (eig_act_ref, eig_grad_ref)

    loads = []
    for at, (src, dst) in enumerate(((query_act_hbm, query_act), (query_grad_hbm, query_grad))):
        loads.append(pltpu.make_async_copy(src, dst, load_sem.at[at]))
    pieces = []
    for kind, (src, dst) in enumerate(((basis_act_hbm, basis_act), (basis_grad_hbm, basis_grad))):
        for row in range(0, src.shape[0], PIECE):
            cut = pl.ds(row, PIECE)
            copy = pltpu.make_async_copy(src.at[cut], dst.at[cut], basis_sem.at[len(pieces)])
            pieces.append((kind, row, copy))
    for at, (src, dst) in enumerate(((token_act_hbm, token_act), (token_grad_hbm, token_grad))):
        loads.append(pltpu.make_async_copy(src, dst, load_sem.at[2 + at]))
    for copy in loads[:2] + [p[2] for p in pieces] + loads[2:]:
        copy.start()

    barrier = pltpu.get_barrier_semaphore()

    def greet(j, carry):
        pl.semaphore_signal(barrier, inc=1, device_id=(g, lax.rem(me + j, n)), device_id_type=MESH)
        return carry

    lax.fori_loop(1, n, greet, 0)

    def device(a_, b_, core_):
        return (g, (a_ * B + b_) * 2 + core_)

    peer = device(a, b, other)
    ys = [device(a, lax.rem(b + i, B), core) for i in range(B)]
    zs = [device(lax.rem(a + j, A), b, core) for j in range(A)]

    def lanes(at, t):
        return pl.ds(pl.multiple_of(at + t * LANES, LANES), LANES)

    def strip_loop(strips, body):
        def run(t, carry):
            body(t)
            return carry

        lax.fori_loop(0, strips, run, 0)

    sizes = []
    for kind in range(2):
        loads[kind].wait()
        query = queries[kind]

        def most(t, carry, query=query):
            return jnp.maximum(carry, jnp.abs(query[:, lanes(0, t)].astype(f32)))

        size = lax.fori_loop(0, query.shape[1] // LANES, most, jnp.zeros((rows, LANES), f32))
        size = jnp.max(size, axis=1, keepdims=True)
        sizes.append(jnp.where(size > 0, size, 1.0))

    for kind in range(2):
        total = jnp.zeros((rows, bases[kind].shape[1]), f32)
        for at_kind, row, copy in pieces:
            if at_kind == kind:
                copy.wait()
                total = total + jnp.dot(
                    queries[kind][:, row : row + PIECE],
                    bases[kind][row : row + PIECE, :],
                    preferred_element_type=f32,
                )
        total = total * (1.0 / (eigs[kind][...] + DAMP)) * (1.0 / sizes[kind])
        high = total.astype(bf16)
        coords[kind][:rows] = high
        coords[kind][rows:] = (total - high.astype(f32)).astype(bf16)
        prods[kind] = jnp.zeros(prods.shape[1:], f32)

    pl.semaphore_wait(barrier, n - 1)
    started = []
    inner = (((1,), (1,)), ((), ()))

    def go(copy):
        copy.start()
        started.append(copy)
        return copy

    def go_pair(q_src, q_dst, s_src, s_dst, sems, at, there):
        q = go(remote(q_src, q_dst, sems.at[(0, 0) + at], sems.at[(1, 0) + at], there))
        s = go(remote(s_src, s_dst, sems.at[(0, 1) + at], sems.at[(1, 1) + at], there))
        return q, s

    def column(core_, b_, k):
        kind, offset, _, _ = chunks[k]
        share = bases[kind].shape[0] // (2 * B)
        return pl.multiple_of((core_ * B + b_) * share + offset, LANES)

    order = [i for i in range(1, B)] + [0]
    core_copies, y_copies, z_copies, az, ay, ac = {}, {}, {}, {}, {}, {}

    def make_part(k):
        kind, _, lane, w = chunks[k]
        cut = pl.ds(lane, w)
        for where, core_ in ((1, other), (0, core)):
            for i in order:
                block = bases[kind][pl.ds(column(core_, lax.rem(b + i, B), k), w), :]
                both = lax.dot_general(coords[kind][...], block, inner, preferred_element_type=f32)
                part[where, i, :, cut] = both[:rows] + both[rows:]
                if where == 1:
                    core_copies[k, i] = go(
                        remote(
                            part.at[1, i, :, cut],
                            core_in.at[i, :, cut],
                            core_sem.at[0, i, k],
                            core_sem.at[1, i, k],
                            peer,
                        )
                    )

    def send_y(k):
        _, _, lane, w = chunks[k]
        cut = pl.ds(lane, w)
        for i in range(1, B):
            core_copies[k, i].wait_recv()

            def body(t, i=i):
                at = lanes(lane, t)
                q, s = quantize(part[0, i, :, at] + core_in[i, :, at])
                y_out[i - 1, :, at] = q
                y_out_s[i - 1, :, at] = s

            strip_loop(w // LANES, body)
            y_copies[k, i] = go_pair(
                y_out.at[i - 1, :, cut],
                y_in.at[i - 1, :, cut],
                y_out_s.at[i - 1, :, cut],
                y_in_s.at[i - 1, :, cut],
                y_sem,
                (i - 1, k),
                ys[i],
            )

    def send_z(k):
        _, _, lane, w = chunks[k]
        cut = pl.ds(lane, w)
        core_copies[k, 0].wait_recv()
        for i in range(1, B):
            for c in y_copies[k, i]:
                c.wait_recv()

        def body(t):
            at = lanes(lane, t)
            total = part[0, 0, :, at] + core_in[0, :, at]
            for i in range(1, B):
                total = total + dequantize(y_in[i - 1, :, at], y_in_s[i - 1, :, at])
            core_in[0, :, at] = total
            for v in range(A):
                q, s = quantize(total[v * R : (v + 1) * R])
                z_out[v, :, at] = q
                z_out_s[v, :, at] = s

        strip_loop(w // LANES, body)
        for j in range(1, A):
            aa = lax.rem(a + j, A)
            z_copies[k, j] = go_pair(
                z_out.at[aa, :, cut],
                z_in.at[j - 1, :, cut],
                z_out_s.at[aa, :, cut],
                z_in_s.at[j - 1, :, cut],
                z_sem,
                (k, j - 1),
                zs[j],
            )

    def send_az(k):
        _, _, lane, w = chunks[k]
        cut = pl.ds(lane, w)
        for j in range(1, A):
            for c in z_copies[k, j]:
                c.wait_recv()
        own = pl.ds(pl.multiple_of(a * R, R), R)

        def body(t):
            at = lanes(lane, t)
            total = core_in[0, own, at]
            for j in range(1, A):
                total = total + dequantize(z_in[j - 1, :, at], z_in_s[j - 1, :, at])
            q, s = quantize(total)
            hat[core, b, a, :, at] = q
            hat_s[core, b, a, :, at] = s

        strip_loop(w // LANES, body)
        q, s = hat.at[core, b, a, :, cut], hat_s.at[core, b, a, :, cut]
        for j in range(1, A):
            az[k, j] = go_pair(q, q, s, s, az_sem, (k, j - 1), zs[j])

    def send_ay(k):
        _, _, lane, w = chunks[k]
        cut = pl.ds(lane, w)
        for j in range(1, A):
            for c in az[k, j]:
                c.wait_recv()
        q, s = hat.at[core, b, :, :, cut], hat_s.at[core, b, :, :, cut]
        for i in range(1, B):
            ay[k, i] = go_pair(q, q, s, s, ay_sem, (k, i - 1), ys[i])
        ac[k, 0] = go_pair(q, q, s, s, ac_sem, (k, 0), peer)

    def send_ac(k):
        _, _, lane, w = chunks[k]
        cut = pl.ds(lane, w)
        for i in range(1, B):
            for c in ay[k, i]:
                c.wait_recv()
            bb = lax.rem(b - i + B, B)
            q, s = hat.at[core, bb, :, :, cut], hat_s.at[core, bb, :, :, cut]
            ac[k, i] = go_pair(q, q, s, s, ac_sem, (k, i), peer)

    def score(k):
        kind, offset, lane, w = chunks[k]
        cut = pl.ds(lane, w)
        share = bases[kind].shape[0] // (2 * B)
        for i in range(B):
            for c in ac[k, i]:
                c.wait_recv()
        if k == 0:
            loads[2].wait()
        if kind == 1 and chunks[k - 1][0] == 0:
            loads[3].wait()
        for h in range(2):
            for bb in range(B):
                value = dequantize(hat[h, bb, :, :, cut], hat_s[h, bb, :, :, cut]).reshape(rows, w)
                high = value.astype(bf16)
                low = (value - high.astype(f32)).astype(bf16)
                start = (h * B + bb) * share + offset
                block = tokens[kind][:, start : start + w]
                prods[kind] += lax.dot_general(
                    jnp.concatenate([high, low], axis=0), block, inner, preferred_element_type=f32
                )

    stages = (make_part, send_y, send_z, send_az, send_ay, send_ac, score)
    for step in range(K + len(stages) - 1):
        for behind, stage in enumerate(stages):
            if 0 <= step - behind < K:
                stage(step - behind)

    docs = mine.shape[0]
    slots = token_act.shape[0]
    place = lax.broadcasted_iota(jnp.int32, (docs, slots), 1)
    which = lax.broadcasted_iota(jnp.int32, (docs, slots), 0)
    member = jnp.zeros((docs, slots), f32)
    begin = jnp.int32(0)
    for d in range(docs):
        length = len_ref[0, me * docs + d]
        inside = (which == d) & (place >= begin) & (place < begin + length)
        member = jnp.where(inside, 1.0 / jnp.full((docs, slots), length, jnp.int32).astype(f32), member)
        begin = begin + length
    prod = [(prods[kind, :rows] + prods[kind, rows:]) * sizes[kind] for kind in range(2)]
    exact = dict(precision=lax.Precision.HIGHEST, preferred_element_type=f32)
    by_row = lax.dot_general(member, prod[0] * prod[1], inner, **exact)
    nq = mine.shape[1]
    row = lax.broadcasted_iota(jnp.int32, (rows, nq), 0)
    first = lax.broadcasted_iota(jnp.int32, (rows, nq), 1) * RANK
    pairs = ((row >= first) & (row < first + RANK)).astype(f32)
    result = jnp.dot(by_row, pairs, **exact)
    mine[...] = result
    every[me] = result

    def copy(j):
        return remote(
            mine, every.at[me], share_sem.at[0, j - 1], share_sem.at[1, j - 1], (g, lax.rem(me + j, n))
        )

    def start(j, carry):
        copy(j).start()
        return carry

    def finish(j, carry):
        copy(j).wait()
        return carry

    lax.fori_loop(1, n, start, 0)
    for c in started:
        c.wait_send()
    lax.fori_loop(1, n, finish, 0)
    table = every[...].reshape(n * docs, nq)
    row = lax.broadcasted_iota(jnp.int32, (docs, n * docs), 0) + me * docs
    pick = (row == owner_ref[...]).astype(f32)
    out_ref[...] = jnp.dot(pick, table, **exact)


def shards(
    doc_len,
    doc_owner,
    query_act,
    query_grad,
    basis_act,
    basis_grad,
    eig_act,
    eig_grad,
    token_act,
    token_grad,
):
    n = lax.axis_size("wide")
    rows = query_act.shape[0]
    B = 2 if n <= 16 else 4
    A = n // (2 * B)
    R = rows // A
    chunks = chunks_of(
        query_act.shape[1] // (2 * B * LANES), query_grad.shape[1] // (2 * B * LANES), MOST_TILES
    )
    K = len(chunks)
    W = chunks[-1][2] + chunks[-1][3]
    docs, nq = doc_len.shape[0] // n, rows // RANK
    slots = token_act.shape[0]
    f32, i16, bf16 = jnp.float32, jnp.int16, jnp.bfloat16
    dma = pltpu.SemaphoreType.DMA
    vmem = pl.BlockSpec(memory_space=pltpu.VMEM)
    anywhere = pl.BlockSpec(memory_space=pl.ANY)
    pieces = (basis_act.shape[0] + basis_grad.shape[0]) // PIECE
    return pl.pallas_call(
        functools.partial(kernel, (n, A, B, R), chunks),
        out_shape=jax.ShapeDtypeStruct((docs, nq), f32),
        in_specs=[pl.BlockSpec(memory_space=pltpu.SMEM), vmem, vmem, vmem] + [anywhere] * 6,
        out_specs=vmem,
        scratch_shapes=[
            pltpu.VMEM(query_act.shape, bf16),
            pltpu.VMEM(query_grad.shape, bf16),
            pltpu.VMEM(basis_act.shape, bf16),
            pltpu.VMEM(basis_grad.shape, bf16),
            pltpu.VMEM(token_act.shape, bf16),
            pltpu.VMEM(token_grad.shape, bf16),
            pltpu.VMEM((2 * rows, basis_act.shape[1]), bf16),
            pltpu.VMEM((2 * rows, basis_grad.shape[1]), bf16),
            pltpu.VMEM((2, B, rows, W), f32),
            pltpu.VMEM((B, rows, W), f32),
            pltpu.VMEM((B - 1, rows, W), i16),
            pltpu.VMEM((B - 1, 1, W), f32),
            pltpu.VMEM((B - 1, rows, W), i16),
            pltpu.VMEM((B - 1, 1, W), f32),
            pltpu.VMEM((A, R, W), i16),
            pltpu.VMEM((A, 1, W), f32),
            pltpu.VMEM((A - 1, R, W), i16),
            pltpu.VMEM((A - 1, 1, W), f32),
            pltpu.VMEM((2, B, A, R, W), i16),
            pltpu.VMEM((2, B, A, 1, W), f32),
            pltpu.VMEM((2, 2 * rows, slots), f32),
            pltpu.VMEM((docs, nq), f32),
            pltpu.VMEM((n, docs, nq), f32),
            dma((4,)),
            dma((pieces,)),
            dma((2, B, K)),
            dma((2, 2, B - 1, K)),
            dma((2, 2, K, A - 1)),
            dma((2, 2, K, A - 1)),
            dma((2, 2, K, B - 1)),
            dma((2, 2, K, B)),
            dma((2, n - 1)),
        ],
        compiler_params=pltpu.CompilerParams(
            collective_id=0, has_side_effects=True, vmem_limit_bytes=56 * 1024 * 1024
        ),
    )(
        doc_len[None, :],
        doc_owner[None, :],
        eig_act[None, :],
        eig_grad[None, :],
        query_act,
        query_grad,
        basis_act,
        basis_grad,
        token_act,
        token_grad,
    )


def solution(mesh):
    placed = (
        P("groups"),
        P("groups"),
        P("groups", None),
        P("groups", None),
        P("groups", "wide"),
        P("groups", "wide"),
        P(("groups", "wide")),
        P(("groups", "wide")),
        P(("groups", "wide"), None),
        P(("groups", "wide"), None),
    )
    return jax.shard_map(
        shards, mesh=mesh, in_specs=placed, out_specs=P(("groups", "wide"), None), check_vma=False
    )
```

```python
import functools

import jax
import jax.numpy as jnp
from jax import lax
from jax.experimental import pallas as pl
from jax.experimental.pallas import tpu as pltpu
from jax.sharding import PartitionSpec as P

RANK = 2
DAMP = 0.1
LANES = 128
LEVELS = 32767.0
LEAST = 1e-34
PIECE = 1024
MOST_TILES = 4
MESH = pl.DeviceIdType.MESH


def remote(src, dst, send, recv, there):
    return pltpu.make_async_remote_copy(
        src_ref=src, dst_ref=dst, send_sem=send, recv_sem=recv, device_id=there, device_id_type=MESH
    )


def quantize(x):
    most = jnp.max(jnp.abs(x), axis=0, keepdims=True)
    up = jnp.where(most > LEAST, LEVELS / jnp.maximum(most, LEAST), 0.0)
    return jnp.round(x * up).astype(jnp.int32).astype(jnp.int16), most * (1.0 / LEVELS)


def dequantize(q, scale):
    return q.astype(jnp.int32).astype(jnp.float32) * scale


def chunks_of(tiles_act, tiles_grad, most):
    chunks, lane = [], 0
    for kind, tiles in ((0, tiles_act), (1, tiles_grad)):
        pieces = -(-tiles // most)
        sizes = [tiles // pieces + (1 if p < tiles % pieces else 0) for p in range(pieces)]
        offset = 0
        for size in sizes:
            chunks.append((kind, offset * LANES, lane * LANES, size * LANES))
            offset += size
            lane += size
    return chunks


def kernel(
    shape,
    chunks,
    len_ref,
    owner_ref,
    eig_act_ref,
    eig_grad_ref,
    query_act_hbm,
    query_grad_hbm,
    basis_act_hbm,
    basis_grad_hbm,
    token_act_hbm,
    token_grad_hbm,
    out_ref,
    query_act,
    query_grad,
    basis_act,
    basis_grad,
    token_act,
    token_grad,
    coords_act,
    coords_grad,
    part,
    core_in,
    y_out,
    y_out_s,
    y_in,
    y_in_s,
    z_out,
    z_out_s,
    z_in,
    z_in_s,
    hat,
    hat_s,
    prods,
    mine,
    every,
    load_sem,
    basis_sem,
    core_sem,
    y_sem,
    z_sem,
    az_sem,
    ay_sem,
    ac_sem,
    share_sem,
):
    n, A, B, R = shape
    K = len(chunks)
    rows = A * R
    f32, bf16 = jnp.float32, jnp.bfloat16
    g = lax.axis_index("groups")
    me = lax.axis_index("wide")
    core = lax.rem(me, 2)
    b = lax.rem(me // 2, B)
    a = me // (2 * B)
    other = 1 - core
    queries = (query_act, query_grad)
    bases = (basis_act, basis_grad)
    tokens = (token_act, token_grad)
    coords = (coords_act, coords_grad)
    eigs = (eig_act_ref, eig_grad_ref)

    loads = []
    for at, (src, dst) in enumerate(((query_act_hbm, query_act), (query_grad_hbm, query_grad))):
        loads.append(pltpu.make_async_copy(src, dst, load_sem.at[at]))
    pieces = []
    for kind, (src, dst) in enumerate(((basis_act_hbm, basis_act), (basis_grad_hbm, basis_grad))):
        for row in range(0, src.shape[kind], PIECE):
            cut = (pl.ds(row, PIECE), slice(None)) if kind == 0 else (slice(None), pl.ds(row, PIECE))
            copy = pltpu.make_async_copy(src.at[cut], dst.at[cut], basis_sem.at[len(pieces)])
            pieces.append((kind, row, copy))
    for at, (src, dst) in enumerate(((token_act_hbm, token_act), (token_grad_hbm, token_grad))):
        loads.append(pltpu.make_async_copy(src, dst, load_sem.at[2 + at]))
    for kind in range(2):
        for copy in [loads[kind]] + [p[2] for p in pieces if p[0] == kind]:
            copy.start()

    barrier = pltpu.get_barrier_semaphore()

    def greet(j, carry):
        pl.semaphore_signal(barrier, inc=1, device_id=(g, lax.rem(me + j, n)), device_id_type=MESH)
        return carry

    lax.fori_loop(1, n, greet, 0)

    def device(a_, b_, core_):
        return (g, (a_ * B + b_) * 2 + core_)

    peer = device(a, b, other)
    ys = [device(a, lax.rem(b + i, B), core) for i in range(B)]
    zs = [device(lax.rem(a + j, A), b, core) for j in range(A)]

    def lanes(at, t):
        return pl.ds(at + t * LANES, LANES)

    def strip_loop(strips, body):
        for t in range(strips):
            body(t)

    inner = (((1,), (1,)), ((), ()))
    sizes = []

    def project(kind):
        loads[kind].wait()
        query = queries[kind]
        most = jnp.zeros((rows, LANES), bf16)
        for at in range(0, query.shape[1], LANES):
            most = jnp.maximum(most, jnp.abs(query[:, at : at + LANES]))
        size = jnp.max(most.astype(f32), axis=1, keepdims=True)
        sizes.append(jnp.where(size > 0, size, 1.0))
        total = jnp.zeros((rows, bases[kind].shape[1 - kind]), f32)
        for at_kind, row, copy in pieces:
            if at_kind == kind:
                copy.wait()
                cut = slice(row, row + PIECE)
                block = query[:, cut]
                if kind == 0:
                    total = total + jnp.dot(block, bases[0][cut, :], preferred_element_type=f32)
                else:
                    total = total + lax.dot_general(block, bases[1][:, cut], inner, preferred_element_type=f32)
        total = total * (1.0 / (eigs[kind][...] + DAMP)) * (1.0 / sizes[kind])
        high = total.astype(bf16)
        coords[kind][:rows] = high
        coords[kind][rows:] = (total - high.astype(f32)).astype(bf16)
        prods[kind] = jnp.zeros(prods.shape[1:], f32)

    project(0)
    pl.semaphore_wait(barrier, n - 1)
    started = []

    def go(copy):
        copy.start()
        started.append(copy)
        return copy

    def go_pair(q_src, q_dst, s_src, s_dst, sems, at, there):
        q = go(remote(q_src, q_dst, sems.at[(0, 0) + at], sems.at[(1, 0) + at], there))
        s = go(remote(s_src, s_dst, sems.at[(0, 1) + at], sems.at[(1, 1) + at], there))
        return q, s

    def column(core_, b_, k):
        kind, offset, _, _ = chunks[k]
        share = tokens[kind].shape[1] // (2 * B)
        return pl.multiple_of((core_ * B + b_) * share + offset, LANES)

    order = [i for i in range(1, B)] + [0]
    core_copies, y_copies, z_copies, az, ay, ac = {}, {}, {}, {}, {}, {}

    def make_part(k):
        kind, _, lane, w = chunks[k]
        cut = pl.ds(lane, w)
        if kind == 1 and chunks[k - 1][0] == 0:
            project(1)
            for copy in loads[2:]:
                copy.start()
        for where, core_ in ((1, other), (0, core)):
            for i in order:
                at = pl.ds(column(core_, lax.rem(b + i, B), k), w)
                if kind == 0:
                    both = lax.dot_general(coords[0][...], bases[0][at, :], inner, preferred_element_type=f32)
                else:
                    both = jnp.dot(coords[1][...], bases[1][:, at], preferred_element_type=f32)
                part[where, i, :, cut] = both[:rows] + both[rows:]
                if where == 1:
                    core_copies[k, i] = go(
                        remote(
                            part.at[1, i, :, cut],
                            core_in.at[i, :, cut],
                            core_sem.at[0, i, k],
                            core_sem.at[1, i, k],
                            peer,
                        )
                    )

    def send_y(k):
        _, _, lane, w = chunks[k]
        cut = pl.ds(lane, w)
        for i in range(1, B):
            core_copies[k, i].wait_recv()

            def body(t, i=i):
                at = lanes(lane, t)
                q, s = quantize(part[0, i, :, at] + core_in[i, :, at])
                y_out[i - 1, :, at] = q
                y_out_s[i - 1, :, at] = s

            strip_loop(w // LANES, body)
            y_copies[k, i] = go_pair(
                y_out.at[i - 1, :, cut],
                y_in.at[i - 1, :, cut],
                y_out_s.at[i - 1, :, cut],
                y_in_s.at[i - 1, :, cut],
                y_sem,
                (i - 1, k),
                ys[i],
            )

    def send_z(k):
        _, _, lane, w = chunks[k]
        cut = pl.ds(lane, w)
        core_copies[k, 0].wait_recv()
        for i in range(1, B):
            for c in y_copies[k, i]:
                c.wait_recv()

        def body(t):
            at = lanes(lane, t)
            total = part[0, 0, :, at] + core_in[0, :, at]
            for i in range(1, B):
                total = total + dequantize(y_in[i - 1, :, at], y_in_s[i - 1, :, at])
            core_in[0, :, at] = total
            for v in range(A):
                q, s = quantize(total[v * R : (v + 1) * R])
                z_out[v, :, at] = q
                z_out_s[v, :, at] = s

        strip_loop(w // LANES, body)
        for j in range(1, A):
            aa = lax.rem(a + j, A)
            z_copies[k, j] = go_pair(
                z_out.at[aa, :, cut],
                z_in.at[j - 1, :, cut],
                z_out_s.at[aa, :, cut],
                z_in_s.at[j - 1, :, cut],
                z_sem,
                (k, j - 1),
                zs[j],
            )

    def send_az(k):
        _, _, lane, w = chunks[k]
        cut = pl.ds(lane, w)
        for j in range(1, A):
            for c in z_copies[k, j]:
                c.wait_recv()
        own = pl.ds(pl.multiple_of(a * R, R), R)

        def body(t):
            at = lanes(lane, t)
            total = core_in[0, own, at]
            for j in range(1, A):
                total = total + dequantize(z_in[j - 1, :, at], z_in_s[j - 1, :, at])
            q, s = quantize(total)
            hat[core, b, a, :, at] = q
            hat_s[core, b, a, :, at] = s

        strip_loop(w // LANES, body)
        q, s = hat.at[core, b, a, :, cut], hat_s.at[core, b, a, :, cut]
        for j in range(1, A):
            az[k, j] = go_pair(q, q, s, s, az_sem, (k, j - 1), zs[j])

    def send_ay(k):
        _, _, lane, w = chunks[k]
        cut = pl.ds(lane, w)
        for j in range(1, A):
            for c in az[k, j]:
                c.wait_recv()
        q, s = hat.at[core, b, :, :, cut], hat_s.at[core, b, :, :, cut]
        for i in range(1, B):
            ay[k, i] = go_pair(q, q, s, s, ay_sem, (k, i - 1), ys[i])
        ac[k, 0] = go_pair(q, q, s, s, ac_sem, (k, 0), peer)

    def send_ac(k):
        _, _, lane, w = chunks[k]
        cut = pl.ds(lane, w)
        for i in range(1, B):
            for c in ay[k, i]:
                c.wait_recv()
            bb = lax.rem(b - i + B, B)
            q, s = hat.at[core, bb, :, :, cut], hat_s.at[core, bb, :, :, cut]
            ac[k, i] = go_pair(q, q, s, s, ac_sem, (k, i), peer)

    def score(k):
        kind, offset, lane, w = chunks[k]
        cut = pl.ds(lane, w)
        share = tokens[kind].shape[1] // (2 * B)
        for i in range(B):
            for c in ac[k, i]:
                c.wait_recv()
        if k == 0:
            loads[2].wait()
        if kind == 1 and chunks[k - 1][0] == 0:
            loads[3].wait()
        for h in range(2):
            for bb in range(B):
                value = dequantize(hat[h, bb, :, :, cut], hat_s[h, bb, :, :, cut]).reshape(rows, w)
                high = value.astype(bf16)
                low = (value - high.astype(f32)).astype(bf16)
                start = (h * B + bb) * share + offset
                block = tokens[kind][:, start : start + w]
                prods[kind] += lax.dot_general(
                    jnp.concatenate([high, low], axis=0), block, inner, preferred_element_type=f32
                )

    stages = (make_part, send_y, send_z, send_az, send_ay, send_ac, score)
    for step in range(K + len(stages) - 1):
        for behind, stage in enumerate(stages):
            if 0 <= step - behind < K:
                stage(step - behind)

    docs = mine.shape[0]
    slots = token_act.shape[0]
    place = lax.broadcasted_iota(jnp.int32, (docs, slots), 1)
    which = lax.broadcasted_iota(jnp.int32, (docs, slots), 0)
    member = jnp.zeros((docs, slots), f32)
    begin = jnp.int32(0)
    for d in range(docs):
        length = len_ref[0, me * docs + d]
        inside = (which == d) & (place >= begin) & (place < begin + length)
        member = jnp.where(inside, 1.0 / jnp.full((docs, slots), length, jnp.int32).astype(f32), member)
        begin = begin + length
    prod = [(prods[kind, :rows] + prods[kind, rows:]) * sizes[kind] for kind in range(2)]
    exact = dict(precision=lax.Precision.HIGHEST, preferred_element_type=f32)
    by_row = lax.dot_general(member, prod[0] * prod[1], inner, **exact)
    nq = mine.shape[1]
    row = lax.broadcasted_iota(jnp.int32, (rows, nq), 0)
    first = lax.broadcasted_iota(jnp.int32, (rows, nq), 1) * RANK
    pairs = ((row >= first) & (row < first + RANK)).astype(f32)
    result = jnp.dot(by_row, pairs, **exact)
    mine[...] = result
    every[me] = result

    def copy(j):
        return remote(
            mine, every.at[me], share_sem.at[0, j - 1], share_sem.at[1, j - 1], (g, lax.rem(me + j, n))
        )

    def start(j, carry):
        copy(j).start()
        return carry

    def finish(j, carry):
        copy(j).wait()
        return carry

    lax.fori_loop(1, n, start, 0)
    for c in started:
        c.wait_send()
    lax.fori_loop(1, n, finish, 0)
    table = every[...].reshape(n * docs, nq)
    row = lax.broadcasted_iota(jnp.int32, (docs, n * docs), 0) + me * docs
    pick = (row == owner_ref[...]).astype(f32)
    out_ref[...] = jnp.dot(pick, table, **exact)


def shards(
    doc_len,
    doc_owner,
    query_act,
    query_grad,
    basis_act,
    basis_grad,
    eig_act,
    eig_grad,
    token_act,
    token_grad,
):
    n = lax.axis_size("wide")
    rows = query_act.shape[0]
    B = 2 if n <= 16 else 4
    A = n // (2 * B)
    R = rows // A
    chunks = chunks_of(
        query_act.shape[1] // (2 * B * LANES), query_grad.shape[1] // (2 * B * LANES), MOST_TILES
    )
    K = len(chunks)
    W = chunks[-1][2] + chunks[-1][3]
    docs, nq = doc_len.shape[0] // n, rows // RANK
    slots = token_act.shape[0]
    f32, i16, bf16 = jnp.float32, jnp.int16, jnp.bfloat16
    dma = pltpu.SemaphoreType.DMA
    vmem = pl.BlockSpec(memory_space=pltpu.VMEM)
    anywhere = pl.BlockSpec(memory_space=pl.ANY)
    pieces = (query_act.shape[1] + query_grad.shape[1]) // PIECE
    return pl.pallas_call(
        functools.partial(kernel, (n, A, B, R), chunks),
        out_shape=jax.ShapeDtypeStruct((docs, nq), f32),
        in_specs=[pl.BlockSpec(memory_space=pltpu.SMEM), vmem, vmem, vmem] + [anywhere] * 6,
        out_specs=vmem,
        scratch_shapes=[
            pltpu.VMEM(query_act.shape, bf16),
            pltpu.VMEM(query_grad.shape, bf16),
            pltpu.VMEM(basis_act.shape, bf16),
            pltpu.VMEM(basis_grad.shape[::-1], bf16),
            pltpu.VMEM(token_act.shape, bf16),
            pltpu.VMEM(token_grad.shape, bf16),
            pltpu.VMEM((2 * rows, basis_act.shape[1]), bf16),
            pltpu.VMEM((2 * rows, basis_grad.shape[1]), bf16),
            pltpu.VMEM((2, B, rows, W), f32),
            pltpu.VMEM((B, rows, W), f32),
            pltpu.VMEM((B - 1, rows, W), i16),
            pltpu.VMEM((B - 1, 1, W), f32),
            pltpu.VMEM((B - 1, rows, W), i16),
            pltpu.VMEM((B - 1, 1, W), f32),
            pltpu.VMEM((A, R, W), i16),
            pltpu.VMEM((A, 1, W), f32),
            pltpu.VMEM((A - 1, R, W), i16),
            pltpu.VMEM((A - 1, 1, W), f32),
            pltpu.VMEM((2, B, A, R, W), i16),
            pltpu.VMEM((2, B, A, 1, W), f32),
            pltpu.VMEM((2, 2 * rows, slots), f32),
            pltpu.VMEM((docs, nq), f32),
            pltpu.VMEM((n, docs, nq), f32),
            dma((4,)),
            dma((pieces,)),
            dma((2, B, K)),
            dma((2, 2, B - 1, K)),
            dma((2, 2, K, A - 1)),
            dma((2, 2, K, A - 1)),
            dma((2, 2, K, B - 1)),
            dma((2, 2, K, B)),
            dma((2, n - 1)),
        ],
        compiler_params=pltpu.CompilerParams(
            collective_id=0, has_side_effects=True, vmem_limit_bytes=56 * 1024 * 1024
        ),
    )(
        doc_len[None, :],
        doc_owner[None, :],
        eig_act[None, :],
        eig_grad[None, :],
        query_act,
        query_grad,
        basis_act,
        basis_grad.T,
        token_act,
        token_grad,
    )


def solution(mesh):
    placed = (
        P("groups"),
        P("groups"),
        P("groups", None),
        P("groups", None),
        P("groups", "wide"),
        P("groups", "wide"),
        P(("groups", "wide")),
        P(("groups", "wide")),
        P(("groups", "wide"), None),
        P(("groups", "wide"), None),
    )
    return jax.shard_map(
        shards, mesh=mesh, in_specs=placed, out_specs=P(("groups", "wide"), None), check_vma=False
    )
```

```python
import functools

import jax
import jax.numpy as jnp
from jax import lax
from jax.experimental import pallas as pl
from jax.experimental.pallas import tpu as pltpu
from jax.sharding import PartitionSpec as P

RANK = 2
DAMP = 0.1
LANES = 128
LEVELS = 32767.0
LEAST = 1e-34
PIECE = 1024
MOST_TILES = 4
MESH = pl.DeviceIdType.MESH


def remote(src, dst, send, recv, there):
    return pltpu.make_async_remote_copy(
        src_ref=src, dst_ref=dst, send_sem=send, recv_sem=recv, device_id=there, device_id_type=MESH
    )


def quantize(x):
    most = jnp.max(jnp.abs(x), axis=0, keepdims=True)
    up = jnp.where(most > LEAST, LEVELS / jnp.maximum(most, LEAST), 0.0)
    return jnp.round(x * up).astype(jnp.int32).astype(jnp.int16), most * (1.0 / LEVELS)


def dequantize(q, scale):
    return q.astype(jnp.int32).astype(jnp.float32) * scale


def chunks_of(tiles_act, tiles_grad, most):
    chunks, lane = [], 0
    for kind, tiles in ((0, tiles_act), (1, tiles_grad)):
        pieces = -(-tiles // most)
        sizes = [tiles // pieces + (1 if p < tiles % pieces else 0) for p in range(pieces)]
        offset = 0
        for size in sizes:
            chunks.append((kind, offset * LANES, lane * LANES, size * LANES))
            offset += size
            lane += size
    return chunks


def kernel(
    shape,
    chunks,
    len_ref,
    owner_ref,
    eig_act_ref,
    eig_grad_ref,
    query_act_hbm,
    query_grad_hbm,
    basis_act_hbm,
    basis_grad_hbm,
    token_act_hbm,
    token_grad_hbm,
    out_ref,
    query_act,
    query_grad,
    basis_act,
    basis_grad,
    token_act,
    token_grad,
    coords_act,
    coords_grad,
    part,
    core_in,
    y_out,
    y_out_s,
    y_in,
    y_in_s,
    z_out,
    z_out_s,
    z_in,
    z_in_s,
    hat,
    hat_s,
    prods,
    mine,
    every,
    load_sem,
    basis_sem,
    core_sem,
    y_sem,
    z_sem,
    az_sem,
    ay_sem,
    ac_sem,
    share_sem,
):
    n, A, B, R = shape
    K = len(chunks)
    rows = A * R
    f32, bf16 = jnp.float32, jnp.bfloat16
    g = lax.axis_index("groups")
    me = lax.axis_index("wide")
    core = lax.rem(me, 2)
    b = lax.rem(me // 2, B)
    a = me // (2 * B)
    other = 1 - core
    queries = (query_act, query_grad)
    bases = (basis_act, basis_grad)
    tokens = (token_act, token_grad)
    coords = (coords_act, coords_grad)
    eigs = (eig_act_ref, eig_grad_ref)

    loads = []
    for at, (src, dst) in enumerate(((query_act_hbm, query_act), (query_grad_hbm, query_grad))):
        loads.append(pltpu.make_async_copy(src, dst, load_sem.at[at]))
    pieces = []
    for kind, (src, dst) in enumerate(((basis_act_hbm, basis_act), (basis_grad_hbm, basis_grad))):
        for row in range(0, src.shape[kind], PIECE):
            cut = (pl.ds(row, PIECE), slice(None)) if kind == 0 else (slice(None), pl.ds(row, PIECE))
            copy = pltpu.make_async_copy(src.at[cut], dst.at[cut], basis_sem.at[len(pieces)])
            pieces.append((kind, row, copy))
    for at, (src, dst) in enumerate(((token_act_hbm, token_act), (token_grad_hbm, token_grad))):
        loads.append(pltpu.make_async_copy(src, dst, load_sem.at[2 + at]))
    for kind in range(2):
        for copy in [loads[kind]] + [p[2] for p in pieces if p[0] == kind]:
            copy.start()

    barrier = pltpu.get_barrier_semaphore()

    def greet(j, carry):
        pl.semaphore_signal(barrier, inc=1, device_id=(g, lax.rem(me + j, n)), device_id_type=MESH)
        return carry

    lax.fori_loop(1, n, greet, 0)

    def device(a_, b_, core_):
        return (g, (a_ * B + b_) * 2 + core_)

    peer = device(a, b, other)
    ys = [device(a, lax.rem(b + i, B), core) for i in range(B)]
    zs = [device(lax.rem(a + j, A), b, core) for j in range(A)]

    def lanes(at, t):
        return pl.ds(at + t * LANES, LANES)

    def strip_loop(strips, body):
        for t in range(strips):
            body(t)

    inner = (((1,), (1,)), ((), ()))
    sizes = []

    def project(kind):
        loads[kind].wait()
        query = queries[kind]
        most = jnp.zeros((rows, LANES), bf16)
        for at in range(0, query.shape[1], LANES):
            most = jnp.maximum(most, jnp.abs(query[:, at : at + LANES]))
        size = jnp.max(most.astype(f32), axis=1, keepdims=True)
        sizes.append(jnp.where(size > 0, size, 1.0))
        total = jnp.zeros((rows, bases[kind].shape[1 - kind]), f32)
        for at_kind, row, copy in pieces:
            if at_kind == kind:
                copy.wait()
                cut = slice(row, row + PIECE)
                block = query[:, cut]
                if kind == 0:
                    total = total + jnp.dot(block, bases[0][cut, :], preferred_element_type=f32)
                else:
                    total = total + lax.dot_general(block, bases[1][:, cut], inner, preferred_element_type=f32)
        total = total * (1.0 / (eigs[kind][...] + DAMP)) * (1.0 / sizes[kind])
        high = total.astype(bf16)
        coords[kind][:rows] = high
        coords[kind][rows:] = (total - high.astype(f32)).astype(bf16)
        prods[kind] = jnp.zeros(prods.shape[1:], f32)

    project(0)
    pl.semaphore_wait(barrier, n - 1)
    started = []

    def go(copy):
        copy.start()
        started.append(copy)
        return copy

    def go_pair(q_src, q_dst, s_src, s_dst, sems, at, there):
        q = go(remote(q_src, q_dst, sems.at[(0, 0) + at], sems.at[(1, 0) + at], there))
        s = go(remote(s_src, s_dst, sems.at[(0, 1) + at], sems.at[(1, 1) + at], there))
        return q, s

    def column(core_, b_, k):
        kind, offset, _, _ = chunks[k]
        share = tokens[kind].shape[1] // (2 * B)
        return pl.multiple_of((core_ * B + b_) * share + offset, LANES)

    order = [i for i in range(1, B)] + [0]
    core_copies, y_copies, z_copies, az, ay, ac = {}, {}, {}, {}, {}, {}

    def make_part(k):
        kind, _, lane, w = chunks[k]
        cut = pl.ds(lane, w)
        if kind == 1 and chunks[k - 1][0] == 0:
            project(1)
            for copy in loads[2:]:
                copy.start()
        for where, core_ in ((1, other), (0, core)):
            for i in order:
                at = pl.ds(column(core_, lax.rem(b + i, B), k), w)
                if kind == 0:
                    both = lax.dot_general(coords[0][...], bases[0][at, :], inner, preferred_element_type=f32)
                else:
                    both = jnp.dot(coords[1][...], bases[1][:, at], preferred_element_type=f32)
                part[where, i, :, cut] = both[:rows] + both[rows:]
                if where == 1:
                    core_copies[k, i] = go(
                        remote(
                            part.at[1, i, :, cut],
                            core_in.at[i, :, cut],
                            core_sem.at[0, i, k],
                            core_sem.at[1, i, k],
                            peer,
                        )
                    )

    def send_y(k):
        _, _, lane, w = chunks[k]
        cut = pl.ds(lane, w)
        for i in range(1, B):
            core_copies[k, i].wait_recv()

            def body(t, i=i):
                at = lanes(lane, t)
                q, s = quantize(part[0, i, :, at] + core_in[i, :, at])
                y_out[i - 1, :, at] = q
                y_out_s[i - 1, :, at] = s

            strip_loop(w // LANES, body)
            y_copies[k, i] = go_pair(
                y_out.at[i - 1, :, cut],
                y_in.at[i - 1, :, cut],
                y_out_s.at[i - 1, :, cut],
                y_in_s.at[i - 1, :, cut],
                y_sem,
                (i - 1, k),
                ys[i],
            )

    def send_z(k):
        _, _, lane, w = chunks[k]
        cut = pl.ds(lane, w)
        core_copies[k, 0].wait_recv()
        for i in range(1, B):
            for c in y_copies[k, i]:
                c.wait_recv()

        def body(t):
            at = lanes(lane, t)
            total = part[0, 0, :, at] + core_in[0, :, at]
            for i in range(1, B):
                total = total + dequantize(y_in[i - 1, :, at], y_in_s[i - 1, :, at])
            core_in[0, :, at] = total
            for v in range(A):
                q, s = quantize(total[v * R : (v + 1) * R])
                z_out[v, :, at] = q
                z_out_s[v, :, at] = s

        strip_loop(w // LANES, body)
        for j in range(1, A):
            aa = lax.rem(a + j, A)
            z_copies[k, j] = go_pair(
                z_out.at[aa, :, cut],
                z_in.at[j - 1, :, cut],
                z_out_s.at[aa, :, cut],
                z_in_s.at[j - 1, :, cut],
                z_sem,
                (k, j - 1),
                zs[j],
            )

    def send_az(k):
        _, _, lane, w = chunks[k]
        cut = pl.ds(lane, w)
        for j in range(1, A):
            for c in z_copies[k, j]:
                c.wait_recv()
        own = pl.ds(pl.multiple_of(a * R, R), R)

        def body(t):
            at = lanes(lane, t)
            total = core_in[0, own, at]
            for j in range(1, A):
                total = total + dequantize(z_in[j - 1, :, at], z_in_s[j - 1, :, at])
            q, s = quantize(total)
            hat[core, b, a, :, at] = q
            hat_s[core, b, a, :, at] = s

        strip_loop(w // LANES, body)
        q, s = hat.at[core, b, a, :, cut], hat_s.at[core, b, a, :, cut]
        for j in range(1, A):
            az[k, j] = go_pair(q, q, s, s, az_sem, (k, j - 1), zs[j])

    def send_ay(k):
        _, _, lane, w = chunks[k]
        cut = pl.ds(lane, w)
        for j in range(1, A):
            for c in az[k, j]:
                c.wait_recv()
        q, s = hat.at[core, b, :, :, cut], hat_s.at[core, b, :, :, cut]
        for i in range(1, B):
            ay[k, i] = go_pair(q, q, s, s, ay_sem, (k, i - 1), ys[i])
        ac[k, 0] = go_pair(q, q, s, s, ac_sem, (k, 0), peer)

    def send_ac(k):
        _, _, lane, w = chunks[k]
        cut = pl.ds(lane, w)
        for i in range(1, B):
            for c in ay[k, i]:
                c.wait_recv()
            bb = lax.rem(b - i + B, B)
            q, s = hat.at[core, bb, :, :, cut], hat_s.at[core, bb, :, :, cut]
            ac[k, i] = go_pair(q, q, s, s, ac_sem, (k, i), peer)

    def score(k):
        kind, offset, lane, w = chunks[k]
        cut = pl.ds(lane, w)
        share = tokens[kind].shape[1] // (2 * B)
        for i in range(B):
            for c in ac[k, i]:
                c.wait_recv()
        if k == 0:
            loads[2].wait()
        if kind == 1 and chunks[k - 1][0] == 0:
            loads[3].wait()
        for h in range(2):
            for bb in range(B):
                value = dequantize(hat[h, bb, :, :, cut], hat_s[h, bb, :, :, cut]).reshape(rows, w)
                high = value.astype(bf16)
                low = (value - high.astype(f32)).astype(bf16)
                start = (h * B + bb) * share + offset
                block = tokens[kind][:, start : start + w]
                prods[kind] += lax.dot_general(
                    jnp.concatenate([high, low], axis=0), block, inner, preferred_element_type=f32
                )

    stages = (make_part, send_y, send_z, send_az, send_ay, send_ac, score)
    for step in range(K + len(stages) - 1):
        for behind in (1, 0, 2, 3, 4, 5, 6):
            stage = stages[behind]
            if 0 <= step - behind < K:
                stage(step - behind)

    docs = mine.shape[0]
    slots = token_act.shape[0]
    place = lax.broadcasted_iota(jnp.int32, (docs, slots), 1)
    which = lax.broadcasted_iota(jnp.int32, (docs, slots), 0)
    member = jnp.zeros((docs, slots), f32)
    begin = jnp.int32(0)
    for d in range(docs):
        length = len_ref[0, me * docs + d]
        inside = (which == d) & (place >= begin) & (place < begin + length)
        member = jnp.where(inside, 1.0 / jnp.full((docs, slots), length, jnp.int32).astype(f32), member)
        begin = begin + length
    prod = [(prods[kind, :rows] + prods[kind, rows:]) * sizes[kind] for kind in range(2)]
    exact = dict(precision=lax.Precision.HIGHEST, preferred_element_type=f32)
    by_row = lax.dot_general(member, prod[0] * prod[1], inner, **exact)
    nq = mine.shape[1]
    row = lax.broadcasted_iota(jnp.int32, (rows, nq), 0)
    first = lax.broadcasted_iota(jnp.int32, (rows, nq), 1) * RANK
    pairs = ((row >= first) & (row < first + RANK)).astype(f32)
    result = jnp.dot(by_row, pairs, **exact)
    mine[...] = result
    every[me] = result

    def copy(j):
        return remote(
            mine, every.at[me], share_sem.at[0, j - 1], share_sem.at[1, j - 1], (g, lax.rem(me + j, n))
        )

    def start(j, carry):
        copy(j).start()
        return carry

    def finish(j, carry):
        copy(j).wait()
        return carry

    lax.fori_loop(1, n, start, 0)
    for c in started:
        c.wait_send()
    lax.fori_loop(1, n, finish, 0)
    table = every[...].reshape(n * docs, nq)
    row = lax.broadcasted_iota(jnp.int32, (docs, n * docs), 0) + me * docs
    pick = (row == owner_ref[...]).astype(f32)
    out_ref[...] = jnp.dot(pick, table, **exact)


def shards(
    doc_len,
    doc_owner,
    query_act,
    query_grad,
    basis_act,
    basis_grad,
    eig_act,
    eig_grad,
    token_act,
    token_grad,
):
    n = lax.axis_size("wide")
    rows = query_act.shape[0]
    B = 2 if n <= 16 else 4
    A = n // (2 * B)
    R = rows // A
    chunks = chunks_of(
        query_act.shape[1] // (2 * B * LANES), query_grad.shape[1] // (2 * B * LANES), MOST_TILES
    )
    K = len(chunks)
    W = chunks[-1][2] + chunks[-1][3]
    docs, nq = doc_len.shape[0] // n, rows // RANK
    slots = token_act.shape[0]
    f32, i16, bf16 = jnp.float32, jnp.int16, jnp.bfloat16
    dma = pltpu.SemaphoreType.DMA
    vmem = pl.BlockSpec(memory_space=pltpu.VMEM)
    anywhere = pl.BlockSpec(memory_space=pl.ANY)
    pieces = (query_act.shape[1] + query_grad.shape[1]) // PIECE
    return pl.pallas_call(
        functools.partial(kernel, (n, A, B, R), chunks),
        out_shape=jax.ShapeDtypeStruct((docs, nq), f32),
        in_specs=[pl.BlockSpec(memory_space=pltpu.SMEM), vmem, vmem, vmem] + [anywhere] * 6,
        out_specs=vmem,
        scratch_shapes=[
            pltpu.VMEM(query_act.shape, bf16),
            pltpu.VMEM(query_grad.shape, bf16),
            pltpu.VMEM(basis_act.shape, bf16),
            pltpu.VMEM(basis_grad.shape[::-1], bf16),
            pltpu.VMEM(token_act.shape, bf16),
            pltpu.VMEM(token_grad.shape, bf16),
            pltpu.VMEM((2 * rows, basis_act.shape[1]), bf16),
            pltpu.VMEM((2 * rows, basis_grad.shape[1]), bf16),
            pltpu.VMEM((2, B, rows, W), f32),
            pltpu.VMEM((B, rows, W), f32),
            pltpu.VMEM((B - 1, rows, W), i16),
            pltpu.VMEM((B - 1, 1, W), f32),
            pltpu.VMEM((B - 1, rows, W), i16),
            pltpu.VMEM((B - 1, 1, W), f32),
            pltpu.VMEM((A, R, W), i16),
            pltpu.VMEM((A, 1, W), f32),
            pltpu.VMEM((A - 1, R, W), i16),
            pltpu.VMEM((A - 1, 1, W), f32),
            pltpu.VMEM((2, B, A, R, W), i16),
            pltpu.VMEM((2, B, A, 1, W), f32),
            pltpu.VMEM((2, 2 * rows, slots), f32),
            pltpu.VMEM((docs, nq), f32),
            pltpu.VMEM((n, docs, nq), f32),
            dma((4,)),
            dma((pieces,)),
            dma((2, B, K)),
            dma((2, 2, B - 1, K)),
            dma((2, 2, K, A - 1)),
            dma((2, 2, K, A - 1)),
            dma((2, 2, K, B - 1)),
            dma((2, 2, K, B)),
            dma((2, n - 1)),
        ],
        compiler_params=pltpu.CompilerParams(
            collective_id=0, has_side_effects=True, vmem_limit_bytes=56 * 1024 * 1024
        ),
    )(
        doc_len[None, :],
        doc_owner[None, :],
        eig_act[None, :],
        eig_grad[None, :],
        query_act,
        query_grad,
        basis_act,
        basis_grad.T,
        token_act,
        token_grad,
    )


def solution(mesh):
    placed = (
        P("groups"),
        P("groups"),
        P("groups", None),
        P("groups", None),
        P("groups", "wide"),
        P("groups", "wide"),
        P(("groups", "wide")),
        P(("groups", "wide")),
        P(("groups", "wide"), None),
        P(("groups", "wide"), None),
    )
    return jax.shard_map(
        shards, mesh=mesh, in_specs=placed, out_specs=P(("groups", "wide"), None), check_vma=False
    )
```
